32 devices in a mesh: group: 2 (over x), expert: 8 (over z, core), tensor: 2 (over y).
Axes of the slice: x: 2, y: 2, z: 4, core: 2. Of those that a mesh axis runs over, the one named last changes fastest.
Arguments:
- heads_out: bfloat16 [1024, 4096], P(('group', 'expert'), 'tensor'), parts along dimension 0, may hold values from -6 to 6
- out_proj: bfloat16 [4096, 2880], P('tensor'), may hold values from -0.09375 to 0.09375
- norm_gain: float32 [2880], replicated, may hold values from 0.25 to 1.75
- gate_up: bfloat16 [8, 2880, 2, 2880], P('expert', None, None, 'tensor'), may hold values from -0.109375 to 0.109375
- down_proj: bfloat16 [8, 2880, 2880], P('expert', 'tensor'), may hold values from -0.109375 to 0.109375
- routes: int32 [1024, 4], P(('group', 'expert', 'tensor')), parts along dimension 0, may hold values from 0 to 7, all different within a row; in each aligned block of 32 rows (0 to 31, 32 to 63, ...) at most 24 rows name the same one
- gate_weights: float32 [1024, 4], P(('group', 'expert', 'tensor')), parts along dimension 0, may hold values from 0.05 to 0.5
Outputs:
- combined: bfloat16 [1024, 2880], P(('group', 'expert', 'tensor')), parts along dimension 0
The draws below stay inside these ranges and needn't reach their ends.
There are 2 independent parts, one for each index of `group`. The reference program is written for one: setup_inputs(seed, part) draws one part's arguments, and reference() takes and returns one part's arrays. A program takes and returns all parts, laid end to end along the dimension named above; an argument that names none is the same for every part. Nothing has to cross between parts.
Inputs may be any that keep to these rules, and one draw needn't show every extreme that they name: `routes`: each row names 4 different experts. Within the rows of one device (aligned blocks of 32 rows) no expert is named by more than 24 rows, and in every draw some expert is named by exactly 24 rows of some block.
All inputs are finite; a program needn't handle non-finite values.
Results may differ from the reference program's by a relative error of at most 0.02.
Values may be sent and summed in bfloat16 or wider, within the bound.
No kernel may reach another device: no remote copies, remote signals or barrier semaphores. Data moves between devices by JAX's collectives and lax.ppermute only.
A program may use at most 128 MiB of HBM per device.

```python
import math
import jax
import jax.numpy as jnp
import numpy as np
from jax import lax

D = 2880
FF = 2880
HIN = 4096
TOPK = 4
TOK_DEV = 32
HB = 64
TOKENS = 512
EXPERTS = 8
CAP = 24
N_TENSOR = 2


def levels(rng, shape, cuts, least, top_value):
    level, own = 1.0, jax.random.fold_in(rng, 6)
    for dim, shards_of in cuts:
        heights = jnp.exp(jax.random.uniform(jax.random.fold_in(own, dim), (shards_of,), jnp.float32, least / len(cuts), top_value / len(cuts)))
        level = level * jnp.repeat(heights, shape[dim] // shards_of).reshape([-1 if axis == dim else 1 for axis in range(len(shape))])
    return level


def shared_out(rng, own, number, rows, count, top, most, lean):
    ranking = jax.random.permutation(rng, count)
    packed, ordinary = shares(count, rows * top, most, lean, True), shares(count, rows * top, most, lean, False)
    places = jnp.arange(count)

    def named(lengths, turn):
        used = int((lengths > 0).sum())
        fixed = max(1, used // 4)
        passed = fixed + (places - fixed + turn * (used - fixed)) % max(1, count - fixed)
        return jnp.zeros((count,), jnp.int32).at[ranking[jnp.where(places < fixed, places, passed)]].set(jnp.asarray(lengths, jnp.int32))

    lengths = jnp.where(number % 4 == 0, named(packed, number // 4), named(ordinary, number - number // 4 - 1))
    mixed = jax.random.permutation(jax.random.fold_in(own, 3), count)
    giver, taker = mixed[0:count // 2 * 2:2], mixed[1:count // 2 * 2:2]
    slack = jnp.minimum(lengths[giver] - 1, most - lengths[taker]) // 2
    slack = jnp.where((giver == ranking[0]) | (taker == ranking[0]) | (lengths[taker] == 0), 0, jnp.maximum(slack, 0))
    passed = jax.random.randint(jax.random.fold_in(own, 4), (count // 2,), 0, 1 << 20) % (slack + 1)
    lengths = lengths.at[giver].add(-passed).at[taker].add(passed)
    labels = jnp.searchsorted(jnp.cumsum(lengths), jnp.arange(rows * top), side="right").astype(jnp.int32)
    grid = labels.reshape(top, rows).T
    grid = grid[jax.random.permutation(jax.random.fold_in(own, 1), rows)]
    turn = jax.random.randint(jax.random.fold_in(own, 2), (rows, 1), 0, top)
    return jnp.take_along_axis(grid, (jnp.arange(top)[None, :] + turn) % top, axis=1)


def shares(count, total, most, lean, full):
    portions = [(1 << 20) // math.isqrt(standing ** lean) + 1 for standing in range(1, count + 1)]
    largest = most if full else min(most, max(-(-total // count), total * portions[0] // sum(portions)))
    least = 1 if total - largest >= count - 1 else 0
    counts, surplus = [largest] + [least] * (count - 1), total - largest - least * (count - 1)
    while surplus > 0:
        free = [i for i in range(1, count) if counts[i] < largest] or [i for i in range(1, count) if counts[i] < most]
        whole, remaining = sum([portions[i] for i in free]), surplus
        for i in free:
            extra = min(most - counts[i], max(1, remaining * portions[i] // whole), surplus)
            counts[i] = counts[i] + extra
            surplus = surplus - extra
    return np.array(counts)


def normal_values(key, extent, width, bound, split=(), held_as=jnp.bfloat16):
    drawn = jax.random.normal(key, extent, jnp.float32) * width
    if len(split) > 0:
        drawn = levels(key, extent, split, -0.22, 0.18) * drawn
    return jnp.clip(drawn, min=-bound, max=bound).astype(held_as)


def setup_inputs(seed: int = 0, part: int = 0) -> dict:
    seeds = jax.random.split(jax.random.key(seed), 8)
    part_splits = jax.random.split(jax.random.fold_in(seeds[7], part), 8)
    heads_out = normal_values(part_splits[0], (TOKENS, HIN), 1.0, 6.0, ((0, 8), (1, 2)))
    out_proj = normal_values(seeds[1], (HIN, D), HIN ** -0.5, 0.09375, ((0, 2),))
    norm_gain = jnp.clip(1.0 + 0.15 * jax.random.normal(seeds[2], (D,), jnp.float32), 0.25, 1.75)
    gate_up = normal_values(seeds[3], (EXPERTS, D, 2, FF), D ** -0.5, 0.109375, ((0, 8), (3, 2)))
    down_proj = normal_values(seeds[4], (EXPERTS, FF, D), FF ** -0.5, 0.109375, ((0, 8), (1, 2)))
    routes_keys = jax.random.split(jax.random.fold_in(part_splits[5], 1), TOKENS // TOK_DEV)
    routes_turns = jax.random.permutation(jax.random.fold_in(part_splits[5], 3), TOKENS // TOK_DEV)
    routes = jax.vmap(lambda own, number: shared_out(jax.random.fold_in(part_splits[5], 2), own, number, TOK_DEV, EXPERTS, TOPK, CAP, 2))(routes_keys, routes_turns).reshape((TOKENS, TOPK))
    gate_weights = jnp.clip(0.05 + 0.45 * jax.random.uniform(part_splits[6], (TOKENS, TOPK), jnp.float32) ** levels(part_splits[6], (TOKENS, TOPK), ((0, 16),), -0.2, 0.2), 0.05, 0.5)
    return dict(heads_out=heads_out, out_proj=out_proj, norm_gain=norm_gain, gate_up=gate_up, down_proj=down_proj, routes=routes, gate_weights=gate_weights)


def hadamard(order):
    positions = jnp.arange(order, dtype=jnp.int32)
    common = jnp.bitwise_and(positions[:, None], positions[None, :])
    ones_count = jnp.zeros((order, order), jnp.int32)
    for bit_pos in range(order.bit_length()):
        ones_count = ones_count + jnp.bitwise_and(jnp.right_shift(common, bit_pos), 1)
    parity = 1 - 2 * jnp.bitwise_and(ones_count, 1)
    return parity.astype(jnp.float32) / math.sqrt(order)

def rotate(values, rotation):
    blocks = values.reshape(-1, HB)
    turned = jnp.dot(blocks, rotation, precision=lax.Precision.HIGHEST, preferred_element_type=jnp.float32)
    return turned.reshape(values.shape)

def reference(heads_out, out_proj, norm_gain, gate_up, down_proj, routes, gate_weights):
    hidden = jnp.dot(heads_out, out_proj, preferred_element_type=jnp.float32)
    scale = lax.rsqrt(lax.optimization_barrier(jnp.mean(hidden * hidden, axis=1, keepdims=True)) + 1e-05)
    normed = (hidden * scale * norm_gain).astype(jnp.bfloat16)
    flat_routes = routes.reshape(-1).astype(jnp.int32)
    onehot = (flat_routes[:, None] == jnp.arange(EXPERTS, dtype=jnp.int32)[None, :]).astype(jnp.int32)
    before = jnp.cumsum(onehot, axis=0) - onehot
    slot_rank = lax.optimization_barrier(jnp.sum(before * onehot, axis=1)).astype(jnp.int32)
    owners = (jnp.arange(TOKENS * TOPK, dtype=jnp.int32) // TOPK).astype(jnp.int32)
    longest = TOKENS // TOK_DEV * CAP
    token_table = jnp.zeros((EXPERTS, longest), jnp.int32).at[flat_routes, slot_rank].set(owners)
    weight_table = jnp.zeros((EXPERTS, longest), jnp.float32).at[flat_routes, slot_rank].set(gate_weights.reshape(-1))
    rotation = hadamard(HB)
    units = FF // N_TENSOR

    def one_expert(running, expert_id):
        token_index = token_table[expert_id]
        inputs = normed[token_index]
        weights_in = gate_up[expert_id]
        gate_part = jnp.dot(inputs, weights_in[:, 0, :], preferred_element_type=jnp.float32)
        up_part = jnp.dot(inputs, weights_in[:, 1, :], preferred_element_type=jnp.float32)
        activation = (gate_part * jax.nn.sigmoid(1.702 * gate_part) * (up_part + 1.0)).astype(jnp.bfloat16)
        weights_out = down_proj[expert_id]
        expert_out = jnp.zeros((longest, D), jnp.float32)
        for shard in range(N_TENSOR):
            partial_sum = jnp.dot(activation[:, shard * units:(shard + 1) * units], weights_out[shard * units:(shard + 1) * units], preferred_element_type=jnp.float32).astype(jnp.bfloat16)
            partial_sum = lax.optimization_barrier(partial_sum)
            expert_out = expert_out + partial_sum.astype(jnp.float32)
        rotated = rotate(expert_out, rotation).astype(jnp.bfloat16)
        rotated = lax.optimization_barrier(rotated)
        running = running.at[token_index].add(weight_table[expert_id][:, None] * rotated.astype(jnp.float32))
        return (running, None)
    mixed, _ = lax.scan(one_expert, jnp.zeros((TOKENS, D), jnp.float32), jnp.arange(EXPERTS, dtype=jnp.int32))
    return rotate(mixed, rotation).astype(jnp.bfloat16)
```

```python
import functools

import jax
import jax.numpy as jnp
from jax import lax
from jax.experimental import pallas as pl
from jax.experimental.pallas import tpu as pltpu
from jax.sharding import PartitionSpec as P

F32 = jnp.float32
BF16 = jnp.bfloat16
NT = (((1,), (1,)), ((), ()))


def out_proj_kernel(heads_ref, w_ref, out_ref):
    out_ref[...] = lax.dot_general(
        heads_ref[...], w_ref[...], NT, preferred_element_type=F32
    ).astype(BF16)


def project(heads_out, out_proj_t):
    rows, depth = heads_out.shape
    width = out_proj_t.shape[0]
    return pl.pallas_call(
        out_proj_kernel,
        grid=(pl.cdiv(width, 384),),
        in_specs=[
            pl.BlockSpec((rows, depth), lambda i: (0, 0)),
            pl.BlockSpec((384, depth), lambda i: (i, 0)),
        ],
        out_specs=pl.BlockSpec((rows, 384), lambda i: (0, i)),
        out_shape=jax.ShapeDtypeStruct((rows, width), BF16),
        compiler_params=pltpu.CompilerParams(vmem_limit_bytes=10 * 2**20),
        name="project",
    )(heads_out, out_proj_t)


def norm_kernel(experts, *refs):
    *parts, gain_ref, routes_ref, weights_ref, out_ref = refs
    hidden = parts[0][...].astype(F32)
    for part in parts[1:]:
        hidden = hidden + part[...].astype(F32)
    rows, width = hidden.shape
    scale = lax.rsqrt(jnp.mean(hidden * hidden, axis=1, keepdims=True) + 1e-05)
    out_ref[:, :width] = (hidden * scale * gain_ref[...]).astype(BF16)
    extra = out_ref.shape[1] - width
    column = lax.broadcasted_iota(jnp.int32, (rows, extra), 1)
    expert, term = lax.rem(column, experts), lax.div(column, experts)
    weight = jnp.zeros((rows, extra), F32)
    for k in range(routes_ref.shape[1]):
        weight = weight + jnp.where(routes_ref[:, k : k + 1] == expert, weights_ref[:, k : k + 1], 0.0)
    high = weight.astype(BF16).astype(F32)
    middle = (weight - high).astype(BF16).astype(F32)
    low = weight - high - middle
    out_ref[:, width:] = jnp.where(
        term == 0, high, jnp.where(term == 1, middle, jnp.where(term == 2, low, 0.0))
    ).astype(BF16)


def expert_kernel(experts, pieces, expert_ref, *refs):
    tokens, (w_in_ref, w_out_ref, near_ref, far_ref, act_ref) = refs[:pieces], refs[pieces:]
    hidden, width = w_out_ref.shape
    block = jnp.concatenate([piece[...] for piece in tokens], axis=0)
    x, extra = block[:, :width], block[:, width:].astype(F32)
    column = lax.broadcasted_iota(jnp.int32, extra.shape, 1)
    mine = (lax.rem(column, experts) == expert_ref[0]) & (column < 3 * experts)
    weight = jnp.sum(jnp.where(mine, extra, 0.0), axis=1, keepdims=True)
    step = 480 if hidden % 480 == 0 else hidden
    for start in range(0, hidden, step):
        gate = lax.dot_general(x, w_in_ref[0, start : start + step], NT, preferred_element_type=F32)
        up = lax.dot_general(x, w_in_ref[1, start : start + step], NT, preferred_element_type=F32)
        act = gate * jax.nn.sigmoid(1.702 * gate) * (up + 1.0)
        act_ref[:, start : start + step] = act.astype(BF16)
    out = jnp.dot(act_ref[...], w_out_ref[...], preferred_element_type=F32) * weight
    half = out.shape[0] // 2
    near_ref[...] = out[:half].astype(BF16)
    far_ref[...] = out[half:].astype(BF16)


def expert_chunk(expert, tokens, w_in, w_out, experts):
    rows = sum(piece.shape[0] for piece in tokens)
    hidden, width = w_out.shape
    vmem = pl.BlockSpec(memory_space=pltpu.VMEM)
    half = jax.ShapeDtypeStruct((rows // 2, width), BF16)
    return pl.pallas_call(
        functools.partial(expert_kernel, experts, len(tokens)),
        in_specs=[pl.BlockSpec(memory_space=pltpu.SMEM)] + [vmem] * (len(tokens) + 2),
        out_specs=[vmem, vmem],
        out_shape=[half, half],
        scratch_shapes=[pltpu.VMEM((rows, hidden), BF16)],
        compiler_params=pltpu.CompilerParams(vmem_limit_bytes=24 * 2**20),
        cost_estimate=pl.CostEstimate(
            flops=6 * rows * hidden * width, bytes_accessed=6 * hidden * width, transcendentals=rows * hidden
        ),
        name="expert",
    )(expert, *tokens, w_in, w_out)


def per_device(sizes, heads_out, out_proj, norm_gain, gate_up, down_proj, routes, gate_weights):
    experts, tensors = sizes
    tokens = routes.shape[0]
    width = out_proj.shape[1]
    padded = -(-(width + 3 * experts) // 128) * 128
    expert = lax.axis_index("expert")
    tensor = lax.axis_index("tensor")

    def swap(values, axis, distance):
        pairs = [(i, i ^ distance) for i in range(lax.axis_size(axis))]
        return lax.ppermute(values, axis, pairs)

    partial = project(heads_out, out_proj.T)

    def rows_of(owner):
        return lax.dynamic_slice_in_dim(partial, owner * tokens, tokens, 0)

    parts = [rows_of(tensor)]
    parts += [swap(rows_of(tensor ^ j), "tensor", j) for j in range(1, tensors)]
    own = pl.pallas_call(
        functools.partial(norm_kernel, experts),
        out_shape=jax.ShapeDtypeStruct((tokens, padded), BF16),
        compiler_params=pltpu.CompilerParams(vmem_limit_bytes=8 * 2**20),
        name="norm",
    )(*parts, norm_gain.reshape(1, width), routes, gate_weights)

    w_in = gate_up[0].transpose(1, 2, 0)
    w_out = down_proj[0]
    me = expert.reshape(1)
    arrived = [own] + [swap(own, "expert", 2 * k) for k in range(1, experts // 2)]
    results = []
    for k, block in enumerate(arrived):
        here = [block] + [swap(block, "tensor", j) for j in range(1, tensors)]
        there = [swap(piece, "expert", 1) for piece in here]
        near, far = expert_chunk(me, here + there, w_in, w_out, experts)
        total = near.astype(F32) + swap(far, "expert", 1).astype(F32)
        mine = total[:tokens]
        for j in range(1, tensors):
            mine = mine + swap(
                total[j * tokens : (j + 1) * tokens].astype(BF16), "tensor", j
            ).astype(F32)
        results.append(mine if k == 0 else swap(mine.astype(BF16), "expert", 2 * k).astype(F32))
    return sum(results[1:], results[0]).astype(BF16)


def solution(mesh):
    return jax.shard_map(
        functools.partial(per_device, (mesh.shape["expert"], mesh.shape["tensor"])),
        mesh=mesh,
        in_specs=(
            P(("group", "expert"), "tensor"),
            P("tensor", None),
            P(),
            P("expert", None, None, "tensor"),
            P("expert", "tensor", None),
            P(("group", "expert", "tensor"), None),
            P(("group", "expert", "tensor"), None),
        ),
        out_specs=P(("group", "expert", "tensor"), None),
        check_vma=False,
    )
```

```python
import functools

import jax
import jax.numpy as jnp
from jax import lax
from jax.experimental import pallas as pl
from jax.experimental.pallas import tpu as pltpu
from jax.sharding import PartitionSpec as P

F32 = jnp.float32
BF16 = jnp.bfloat16
NT = (((1,), (1,)), ((), ()))
TN = (((0,), (0,)), ((), ()))

AHEAD = 2
CHEAP = pl.CostEstimate(flops=0, bytes_accessed=0, transcendentals=0)


def project_kernel(tile, tensor_ref, heads_hbm, w_hbm, *refs):
    *part_refs, heads_ref, w_ref, out_ref, heads_sem, sems = refs
    width, depth = w_ref.shape
    first = pltpu.make_async_copy(heads_hbm, heads_ref, heads_sem)
    first.start()
    tiles = [(start, min(tile, width - start)) for start in range(0, width, tile)]
    copies = []
    for i, (start, size) in enumerate(tiles):
        rows = pl.ds(start, size)
        copies.append(pltpu.make_async_copy(w_hbm.at[rows], w_ref.at[rows], sems.at[i]))
    for copy in copies[:AHEAD]:
        copy.start()
    first.wait()
    heads = heads_ref[...]
    for i, (start, size) in enumerate(tiles):
        copies[i].wait()
        if i + AHEAD < len(tiles):
            copies[i + AHEAD].start()
        out = lax.dot_general(heads, w_ref[start : start + size], NT, preferred_element_type=F32)
        out_ref[:, start : start + size] = out.astype(BF16)
    tokens = part_refs[0].shape[0]
    for j, part_ref in enumerate(part_refs):
        start = pl.multiple_of((tensor_ref[0] ^ j) * tokens, tokens)
        part_ref[...] = out_ref[pl.ds(start, tokens)]


def project(tensor, heads_out, out_proj_t, tensors):
    rows, depth = heads_out.shape
    width = out_proj_t.shape[0]
    tile = 384
    hbm = pl.BlockSpec(memory_space=pltpu.HBM)
    part = jax.ShapeDtypeStruct((rows // tensors, width), BF16)
    return pl.pallas_call(
        functools.partial(project_kernel, tile),
        in_specs=[pl.BlockSpec(memory_space=pltpu.SMEM), hbm, hbm],
        out_specs=[pl.BlockSpec(memory_space=pltpu.VMEM)] * tensors,
        out_shape=[part] * tensors,
        scratch_shapes=[
            pltpu.VMEM((rows, depth), BF16),
            pltpu.VMEM((width, depth), BF16),
            pltpu.VMEM((rows, width), BF16),
            pltpu.SemaphoreType.DMA,
            pltpu.SemaphoreType.DMA((pl.cdiv(width, tile),)),
        ],
        compiler_params=pltpu.CompilerParams(vmem_limit_bytes=24 * 2**20),
        cost_estimate=CHEAP,
        name="project",
    )(
        tensor,
        pltpu.with_memory_space_constraint(heads_out, pltpu.HBM),
        pltpu.with_memory_space_constraint(out_proj_t, pltpu.HBM),
    )


def norm_kernel(experts, *refs):
    *parts, gain_ref, routes_ref, weights_ref, _, out_ref = refs
    hidden = parts[0][...].astype(F32)
    for part in parts[1:]:
        hidden = hidden + part[...].astype(F32)
    rows, width = hidden.shape
    scale = lax.rsqrt(jnp.mean(hidden * hidden, axis=1, keepdims=True) + 1e-05)
    out_ref[:, :width] = (hidden * scale * gain_ref[...]).astype(BF16)
    extra = out_ref.shape[1] - width
    column = lax.broadcasted_iota(jnp.int32, (rows, extra), 1)
    expert, term = lax.rem(column, experts), lax.div(column, experts)
    weight = jnp.zeros((rows, extra), F32)
    for k in range(routes_ref.shape[1]):
        weight = weight + jnp.where(routes_ref[:, k : k + 1] == expert, weights_ref[:, k : k + 1], 0.0)
    high = weight.astype(BF16).astype(F32)
    middle = (weight - high).astype(BF16).astype(F32)
    low = weight - high - middle
    out_ref[:, width:] = jnp.where(
        term == 0, high, jnp.where(term == 1, middle, jnp.where(term == 2, low, 0.0))
    ).astype(BF16)


def expert_kernel(experts, pieces, expert_ref, *refs):
    tokens = refs[:pieces]
    w_in_ref, w_out_ref = refs[pieces : pieces + 2]
    near_ref, far_ref, act_ref = refs[-3:]
    hidden, width = w_out_ref.shape
    block = jnp.concatenate([piece[...] for piece in tokens], axis=0)
    x, extra = block[:, :width], block[:, width:].astype(F32)
    column = lax.broadcasted_iota(jnp.int32, extra.shape, 1)
    mine = (lax.rem(column, experts) == expert_ref[0]) & (column < 3 * experts)
    weight = jnp.sum(jnp.where(mine, extra, 0.0), axis=1, keepdims=True)
    step = 480 if hidden % 480 == 0 else hidden
    for start in range(0, hidden, step):
        gate = lax.dot_general(w_in_ref[0, start : start + step], x, NT, preferred_element_type=F32)
        up = lax.dot_general(w_in_ref[1, start : start + step], x, NT, preferred_element_type=F32)
        act = gate * jax.nn.sigmoid(1.702 * gate) * (up + 1.0)
        act_ref[start : start + step, :] = act.astype(BF16)
    out = lax.dot_general(act_ref[...], w_out_ref[...], TN, preferred_element_type=F32) * weight
    half = out.shape[0] // 2
    near_ref[...] = out[:half].astype(BF16).reshape(near_ref.shape)
    far_ref[...] = out[half:].astype(BF16).reshape(far_ref.shape)


def expert_chunk(expert, tokens, w_in, w_out, experts, after):
    rows = sum(piece.shape[0] for piece in tokens)
    hidden, width = w_out.shape
    vmem = pl.BlockSpec(memory_space=pltpu.VMEM)
    unit = tokens[0].shape[0]
    half = jax.ShapeDtypeStruct((rows // 2 // unit, unit, width), BF16)
    return pl.pallas_call(
        functools.partial(expert_kernel, experts, len(tokens)),
        in_specs=[pl.BlockSpec(memory_space=pltpu.SMEM)]
        + [vmem] * (len(tokens) + 2)
        + [pl.BlockSpec(memory_space=pl.ANY)] * len(after),
        out_specs=[vmem, vmem],
        out_shape=[half, half],
        scratch_shapes=[pltpu.VMEM((hidden, rows), BF16)],
        compiler_params=pltpu.CompilerParams(vmem_limit_bytes=24 * 2**20),
        cost_estimate=pl.CostEstimate(
            flops=6 * rows * hidden * width, bytes_accessed=rows * width, transcendentals=rows * hidden
        ),
        name="expert",
    )(
        expert,
        *tokens,
        pltpu.with_memory_space_constraint(w_in, pltpu.VMEM),
        pltpu.with_memory_space_constraint(w_out, pltpu.VMEM),
        *after,
    )


def load_kernel(source_ref, *refs):
    target_ref, token_ref, sem = refs[-3:]
    copy = pltpu.make_async_copy(source_ref, target_ref, sem)
    copy.start()
    token_ref[...] = jnp.zeros_like(token_ref)
    copy.wait()


def load(weights, after):
    return pl.pallas_call(
        load_kernel,
        in_specs=[pl.BlockSpec(memory_space=pltpu.HBM)] + [pl.BlockSpec(memory_space=pl.ANY)] * len(after),
        out_specs=[pl.BlockSpec(memory_space=pltpu.VMEM)] * 2,
        out_shape=[pltpu.VMEM(weights.shape, weights.dtype), jax.ShapeDtypeStruct((8, 128), F32)],
        scratch_shapes=[pltpu.SemaphoreType.DMA],
        compiler_params=pltpu.CompilerParams(vmem_limit_bytes=2**20),
        cost_estimate=pl.CostEstimate(flops=0, bytes_accessed=2 * weights.size, transcendentals=0),
        name="load",
    )(pltpu.with_memory_space_constraint(weights, pltpu.HBM), *after)


def add_kernel(kept, near_ref, far_ref, *out_refs):
    for i, out_ref in enumerate(out_refs):
        total = near_ref[i].astype(F32) + far_ref[i].astype(F32)
        out_ref[...] = total.astype(out_ref.dtype)


def add_split(near, far, kept):
    blocks, *shape = near.shape
    return pl.pallas_call(
        functools.partial(add_kernel, kept),
        out_shape=[jax.ShapeDtypeStruct(shape, F32 if i < kept else BF16) for i in range(blocks)],
        compiler_params=pltpu.CompilerParams(vmem_limit_bytes=16 * 2**20),
        cost_estimate=CHEAP,
        name="add_split",
    )(near, far)


def gate_kernel(count, *refs):
    for source_ref, out_ref in zip(refs[:count], refs[len(refs) - count :]):
        out_ref[...] = source_ref[...]


def gate(values, after):
    vmem = pl.BlockSpec(memory_space=pltpu.VMEM)
    return pl.pallas_call(
        functools.partial(gate_kernel, len(values)),
        in_specs=[vmem] * len(values) + [pl.BlockSpec(memory_space=pl.ANY)] * len(after),
        out_specs=[vmem] * len(values),
        out_shape=[jax.ShapeDtypeStruct(value.shape, value.dtype) for value in values],
        compiler_params=pltpu.CompilerParams(vmem_limit_bytes=4 * 2**20),
        cost_estimate=CHEAP,
        name="gate",
    )(*values, *after)


def sum_kernel(count, *refs):
    total = refs[0][...].astype(F32)
    for term in refs[1:count]:
        total = total + term[...].astype(F32)
    refs[-1][...] = total.astype(refs[-1].dtype)


def add_up(terms, dtype, after=()):
    vmem = pl.BlockSpec(memory_space=pltpu.VMEM)
    return pl.pallas_call(
        functools.partial(sum_kernel, len(terms)),
        in_specs=[vmem] * len(terms) + [pl.BlockSpec(memory_space=pl.ANY)] * len(after),
        out_specs=vmem,
        out_shape=jax.ShapeDtypeStruct(terms[0].shape, dtype),
        compiler_params=pltpu.CompilerParams(vmem_limit_bytes=16 * 2**20),
        cost_estimate=CHEAP,
        name="add_up",
    )(*terms, *after)


def per_device(sizes, heads_out, out_proj, norm_gain, gate_up, down_proj, routes, gate_weights):
    experts, tensors = sizes
    tokens = routes.shape[0]
    width = out_proj.shape[1]
    padded = -(-(width + 3 * experts) // 128) * 128
    expert = lax.axis_index("expert")
    tensor = lax.axis_index("tensor")

    def swap(values, axis, distance):
        pairs = [(i, i ^ distance) for i in range(lax.axis_size(axis))]
        return lax.ppermute(values, axis, pairs)

    mine, *sent = project(tensor.reshape(1), heads_out, out_proj.T, tensors)
    gain = norm_gain.reshape(1, width)
    me = expert.reshape(1)
    w_in, w_in_there = load(gate_up[0].transpose(1, 2, 0), [*sent, gain, routes, gate_weights, me])
    parts = [mine] + [swap(sent[j - 1], "tensor", j) for j in range(1, tensors)]
    own = pl.pallas_call(
        functools.partial(norm_kernel, experts),
        in_specs=[pl.BlockSpec(memory_space=pltpu.VMEM)] * (tensors + 3) + [pl.BlockSpec(memory_space=pl.ANY)],
        out_shape=jax.ShapeDtypeStruct((tokens, padded), BF16),
        compiler_params=pltpu.CompilerParams(vmem_limit_bytes=8 * 2**20),
        name="norm",
    )(*parts, gain, routes, gate_weights, w_in_there)
    w_out, w_out_there = load(down_proj[0], [own])

    chips = experts // 2
    relayed = chips > 3
    order = [0, 1, 3, 2, *range(4, chips)][:chips] if relayed else list(range(chips))
    arrived = {0: own}
    for k in order[1:]:
        if relayed and k == 2:
            arrived[k] = swap(arrived[3], "expert", 2)
        else:
            arrived[k] = swap(own, "expert", 2 * k)
        if relayed and k == 3:
            (arrived[k],) = gate([arrived[k]], [w_out_there])
    chunks = [order[i : i + 2] for i in range(0, chips, 2)]

    def across(k):
        return [arrived[k]] + [swap(arrived[k], "tensor", j) for j in range(1, tensors)]

    here = {k: across(k) for k in order}
    sums, after = {}, ([arrived[2], *here[3][1:]] if relayed else [])
    for number, chunk in enumerate(chunks):
        there = {k: [swap(piece, "expert", 1) for piece in here[k]] for k in chunk}
        ordered = [side[k][j] for side in (here, there) for j in range(tensors) for k in chunk]
        near, far = expert_chunk(me, ordered, w_in, w_out, experts, after)
        after = []
        if number == 0 and len(chunks) > 1:
            last = here[chunks[1][-1]]
            far, *last[1:] = gate([far, *last[1:]], [])
        elif number == 1:
            (far,) = gate([far], sums[chunks[0][-1]][1:])
        count = len(chunk)
        added = add_split(near, swap(far, "expert", 1), count)
        for i, k in enumerate(chunk):
            sums[k] = [added[i], *(swap(added[j * count + i], "tensor", j) for j in range(1, tensors))]

    def back(k, after=()):
        distance = 1 if relayed and k == 3 else k
        return swap(add_up(sums[k], BF16, after), "expert", 2 * distance)

    terms = list(sums[0])
    for k in order[1:]:
        if relayed and k == 3:
            sums[2].append(back(k, terms[-1:]))
        else:
            terms.append(back(k))
    return add_up(terms, BF16)


def solution(mesh):
    return jax.shard_map(
        functools.partial(per_device, (mesh.shape["expert"], mesh.shape["tensor"])),
        mesh=mesh,
        in_specs=(
            P(("group", "expert"), "tensor"),
            P("tensor", None),
            P(),
            P("expert", None, None, "tensor"),
            P("expert", "tensor", None),
            P(("group", "expert", "tensor"), None),
            P(("group", "expert", "tensor"), None),
        ),
        out_specs=P(("group", "expert", "tensor"), None),
        check_vma=False,
    )
```

```python
import functools

import jax
import jax.numpy as jnp
from jax import lax
from jax.experimental import pallas as pl
from jax.experimental.pallas import tpu as pltpu
from jax.sharding import PartitionSpec as P

F32 = jnp.float32
BF16 = jnp.bfloat16
NT = (((1,), (1,)), ((), ()))
TN = (((0,), (0,)), ((), ()))

AHEAD = 2
CHEAP = pl.CostEstimate(flops=0, bytes_accessed=0, transcendentals=0)


def project_kernel(tile, tensor_ref, heads_hbm, w_hbm, *refs):
    *part_refs, heads_ref, w_ref, out_ref, heads_sem, sems = refs
    width, depth = w_ref.shape
    first = pltpu.make_async_copy(heads_hbm, heads_ref, heads_sem)
    first.start()
    tiles = [(start, min(tile, width - start)) for start in range(0, width, tile)]
    copies = []
    for i, (start, size) in enumerate(tiles):
        rows = pl.ds(start, size)
        copies.append(pltpu.make_async_copy(w_hbm.at[rows], w_ref.at[rows], sems.at[i]))
    for copy in copies[:AHEAD]:
        copy.start()
    first.wait()
    heads = heads_ref[...]
    for i, (start, size) in enumerate(tiles):
        copies[i].wait()
        if i + AHEAD < len(tiles):
            copies[i + AHEAD].start()
        out = lax.dot_general(heads, w_ref[start : start + size], NT, preferred_element_type=F32)
        out_ref[:, start : start + size] = out.astype(BF16)
    tokens = part_refs[0].shape[0]
    for j, part_ref in enumerate(part_refs):
        start = pl.multiple_of((tensor_ref[0] ^ j) * tokens, tokens)
        part_ref[...] = out_ref[pl.ds(start, tokens)]


def project(tensor, heads_out, out_proj_t, tensors):
    rows, depth = heads_out.shape
    width = out_proj_t.shape[0]
    tile = 512
    hbm = pl.BlockSpec(memory_space=pltpu.HBM)
    part = jax.ShapeDtypeStruct((rows // tensors, width), BF16)
    return pl.pallas_call(
        functools.partial(project_kernel, tile),
        in_specs=[pl.BlockSpec(memory_space=pltpu.SMEM), hbm, hbm],
        out_specs=[pl.BlockSpec(memory_space=pltpu.VMEM)] * tensors,
        out_shape=[part] * tensors,
        scratch_shapes=[
            pltpu.VMEM((rows, depth), BF16),
            pltpu.VMEM((width, depth), BF16),
            pltpu.VMEM((rows, width), BF16),
            pltpu.SemaphoreType.DMA,
            pltpu.SemaphoreType.DMA((pl.cdiv(width, tile),)),
        ],
        compiler_params=pltpu.CompilerParams(vmem_limit_bytes=24 * 2**20),
        cost_estimate=CHEAP,
        name="project",
    )(
        tensor,
        pltpu.with_memory_space_constraint(heads_out, pltpu.HBM),
        pltpu.with_memory_space_constraint(out_proj_t, pltpu.HBM),
    )


def norm_kernel(experts, *refs):
    *parts, gain_ref, routes_ref, weights_ref, _, out_ref = refs
    hidden = parts[0][...].astype(F32)
    for part in parts[1:]:
        hidden = hidden + part[...].astype(F32)
    rows, width = hidden.shape
    scale = lax.rsqrt(jnp.mean(hidden * hidden, axis=1, keepdims=True) + 1e-05)
    out_ref[:, :width] = (hidden * scale * gain_ref[...]).astype(BF16)
    extra = out_ref.shape[1] - width
    column = lax.broadcasted_iota(jnp.int32, (rows, extra), 1)
    expert, term = lax.rem(column, experts), lax.div(column, experts)
    weight = jnp.zeros((rows, extra), F32)
    for k in range(routes_ref.shape[1]):
        weight = weight + jnp.where(routes_ref[:, k : k + 1] == expert, weights_ref[:, k : k + 1], 0.0)
    high = weight.astype(BF16).astype(F32)
    middle = (weight - high).astype(BF16).astype(F32)
    low = weight - high - middle
    out_ref[:, width:] = jnp.where(
        term == 0, high, jnp.where(term == 1, middle, jnp.where(term == 2, low, 0.0))
    ).astype(BF16)


def expert_kernel(experts, pieces, outputs, expert_ref, *refs):
    tokens = refs[:pieces]
    w_in_ref, w_out_ref = refs[pieces : pieces + 2]
    near_ref, *far_refs, act_ref = refs[outputs:]
    hidden, width = w_out_ref.shape
    block = jnp.concatenate([piece[...] for piece in tokens], axis=0)
    x, extra = block[:, :width], block[:, width:].astype(F32)
    column = lax.broadcasted_iota(jnp.int32, extra.shape, 1)
    mine = (lax.rem(column, experts) == expert_ref[0]) & (column < 3 * experts)
    weight = jnp.sum(jnp.where(mine, extra, 0.0), axis=1, keepdims=True)
    step = 480 if hidden % 480 == 0 else hidden
    for start in range(0, hidden, step):
        gate = lax.dot_general(w_in_ref[0, start : start + step], x, NT, preferred_element_type=F32)
        up = lax.dot_general(w_in_ref[1, start : start + step], x, NT, preferred_element_type=F32)
        act = gate * jax.nn.sigmoid(1.702 * gate) * (up + 1.0)
        act_ref[start : start + step, :] = act.astype(BF16)
    out = lax.dot_general(act_ref[...], w_out_ref[...], TN, preferred_element_type=F32) * weight
    half = out.shape[0] // 2
    near_ref[...] = out[:half].astype(BF16).reshape(near_ref.shape)
    far = out[half:].astype(BF16)
    size = half // len(far_refs)
    for i, far_ref in enumerate(far_refs):
        far_ref[...] = far[i * size : (i + 1) * size].reshape(far_ref.shape)


def expert_chunk(expert, tokens, w_in, w_out, experts, after, split):
    rows = sum(piece.shape[0] for piece in tokens)
    hidden, width = w_out.shape
    vmem = pl.BlockSpec(memory_space=pltpu.VMEM)
    unit = tokens[0].shape[0]
    blocks = rows // 2 // unit
    near = jax.ShapeDtypeStruct((blocks, unit, width), BF16)
    far = [jax.ShapeDtypeStruct((unit, width), BF16)] * blocks if split else [near]
    inputs = len(tokens) + 2 + len(after)
    return pl.pallas_call(
        functools.partial(expert_kernel, experts, len(tokens), inputs),
        in_specs=[pl.BlockSpec(memory_space=pltpu.SMEM)]
        + [vmem] * (len(tokens) + 2)
        + [pl.BlockSpec(memory_space=pl.ANY)] * len(after),
        out_specs=[vmem] * (1 + len(far)),
        out_shape=[near, *far],
        scratch_shapes=[pltpu.VMEM((hidden, rows), BF16)],
        compiler_params=pltpu.CompilerParams(vmem_limit_bytes=24 * 2**20),
        cost_estimate=pl.CostEstimate(
            flops=6 * rows * hidden * width, bytes_accessed=rows * width, transcendentals=rows * hidden
        ),
        name="expert",
    )(
        expert,
        *tokens,
        pltpu.with_memory_space_constraint(w_in, pltpu.VMEM),
        pltpu.with_memory_space_constraint(w_out, pltpu.VMEM),
        *after,
    )


def load_kernel(source_ref, *refs):
    target_ref, token_ref, sem = refs[-3:]
    copy = pltpu.make_async_copy(source_ref, target_ref, sem)
    copy.start()
    token_ref[...] = jnp.zeros_like(token_ref)
    copy.wait()


def load(weights, after):
    return pl.pallas_call(
        load_kernel,
        in_specs=[pl.BlockSpec(memory_space=pltpu.HBM)] + [pl.BlockSpec(memory_space=pl.ANY)] * len(after),
        out_specs=[pl.BlockSpec(memory_space=pltpu.VMEM)] * 2,
        out_shape=[pltpu.VMEM(weights.shape, weights.dtype), jax.ShapeDtypeStruct((8, 128), F32)],
        scratch_shapes=[pltpu.SemaphoreType.DMA],
        compiler_params=pltpu.CompilerParams(vmem_limit_bytes=2**20),
        cost_estimate=pl.CostEstimate(flops=0, bytes_accessed=2 * weights.size, transcendentals=0),
        name="load",
    )(pltpu.with_memory_space_constraint(weights, pltpu.HBM), *after)


def add_kernel(fars, outputs, near_ref, *refs):
    far_refs = refs[:fars]

    def block(i):
        far = far_refs[0][i] if fars == 1 else far_refs[i][...]
        return near_ref[i].astype(F32) + far.astype(F32)

    done = 0
    for out_ref in refs[-outputs:]:
        if len(out_ref.shape) == 2:
            out_ref[...] = block(done).astype(out_ref.dtype)
            done += 1
        else:
            for i in range(out_ref.shape[0]):
                out_ref[i] = block(done).astype(out_ref.dtype)
                done += 1


def add_split(near, fars, kept, after):
    blocks, *shape = near.shape
    vmem = pl.BlockSpec(memory_space=pltpu.VMEM)
    sent = shape if kept == 1 else (kept, *shape)
    shapes = [jax.ShapeDtypeStruct(shape, F32)] * kept + [jax.ShapeDtypeStruct(sent, BF16)] * (blocks // kept - 1)
    return pl.pallas_call(
        functools.partial(add_kernel, len(fars), len(shapes)),
        in_specs=[vmem] * (1 + len(fars)) + [pl.BlockSpec(memory_space=pl.ANY)] * len(after),
        out_specs=[vmem] * len(shapes),
        out_shape=shapes,
        compiler_params=pltpu.CompilerParams(vmem_limit_bytes=16 * 2**20),
        cost_estimate=CHEAP,
        name="add_split",
    )(near, *fars, *after)


def gate_kernel(count, *refs):
    for source_ref, out_ref in zip(refs[:count], refs[len(refs) - count :]):
        out_ref[...] = source_ref[...]


def gate(values, after):
    vmem = pl.BlockSpec(memory_space=pltpu.VMEM)
    return pl.pallas_call(
        functools.partial(gate_kernel, len(values)),
        in_specs=[vmem] * len(values) + [pl.BlockSpec(memory_space=pl.ANY)] * len(after),
        out_specs=[vmem] * len(values),
        out_shape=[jax.ShapeDtypeStruct(value.shape, value.dtype) for value in values],
        compiler_params=pltpu.CompilerParams(vmem_limit_bytes=4 * 2**20),
        cost_estimate=CHEAP,
        name="gate",
    )(*values, *after)


def sum_kernel(places, *refs):
    total = None
    for place, ref in zip(places, refs):
        term = (ref[...] if place is None else ref[place]).astype(F32)
        total = term if total is None else total + term
    refs[-1][...] = total.astype(refs[-1].dtype)


def add_up(terms, dtype, after=()):
    vmem = pl.BlockSpec(memory_space=pltpu.VMEM)
    places = [term[1] if isinstance(term, tuple) else None for term in terms]
    arrays = [term[0] if isinstance(term, tuple) else term for term in terms]
    return pl.pallas_call(
        functools.partial(sum_kernel, places),
        in_specs=[vmem] * len(terms) + [pl.BlockSpec(memory_space=pl.ANY)] * len(after),
        out_specs=vmem,
        out_shape=jax.ShapeDtypeStruct(arrays[0].shape, dtype),
        compiler_params=pltpu.CompilerParams(vmem_limit_bytes=16 * 2**20),
        cost_estimate=CHEAP,
        name="add_up",
    )(*arrays, *after)


def per_device(sizes, heads_out, out_proj, norm_gain, gate_up, down_proj, routes, gate_weights):
    experts, tensors = sizes
    tokens = routes.shape[0]
    width = out_proj.shape[1]
    padded = -(-(width + 3 * experts) // 128) * 128
    expert = lax.axis_index("expert")
    tensor = lax.axis_index("tensor")

    def swap(values, axis, distance):
        pairs = [(i, i ^ distance) for i in range(lax.axis_size(axis))]
        return lax.ppermute(values, axis, pairs)

    mine, *sent = project(tensor.reshape(1), heads_out, out_proj.T, tensors)
    gain = norm_gain.reshape(1, width)
    me = expert.reshape(1)
    w_in, w_in_there = load(gate_up[0].transpose(1, 2, 0), [*sent, gain, routes, gate_weights, me])
    parts = [mine] + [swap(sent[j - 1], "tensor", j) for j in range(1, tensors)]
    own = pl.pallas_call(
        functools.partial(norm_kernel, experts),
        in_specs=[pl.BlockSpec(memory_space=pltpu.VMEM)] * (tensors + 3) + [pl.BlockSpec(memory_space=pl.ANY)],
        out_shape=jax.ShapeDtypeStruct((tokens, padded), BF16),
        compiler_params=pltpu.CompilerParams(vmem_limit_bytes=8 * 2**20),
        name="norm",
    )(*parts, gain, routes, gate_weights, w_in_there)
    w_out, w_out_there = load(down_proj[0], [own])

    chips = experts // 2
    relayed = chips > 3
    order = [0, 1, 3, 2, *range(4, chips)][:chips] if relayed else list(range(chips))
    arrived = {0: own}
    for k in order[1:]:
        if relayed and k == 2:
            arrived[k] = swap(arrived[3], "expert", 2)
        else:
            arrived[k] = swap(own, "expert", 2 * k)
        if k == 1:
            (arrived[k],) = gate([arrived[k]], [w_out_there])
    chunks = [[0], [1, 3], *([k] for k in order[3:])] if relayed else [[k] for k in order]

    def across(k):
        return [arrived[k]] + [swap(arrived[k], "tensor", j) for j in range(1, tensors)]

    here = {k: across(k) for k in order if not relayed or k != 2}
    sums, came, held = {}, {}, {}
    for number, chunk in enumerate(chunks):
        there = {k: [swap(piece, "expert", 1) for piece in here[k]] for k in chunk}
        ordered = [side[k][j] for side in (here, there) for j in range(tensors) for k in chunk]
        after = [arrived[3]] if relayed and number == 0 else []
        near, *far = expert_chunk(me, ordered, w_in, w_out, experts, after, relayed and number == 2)
        last = []
        if relayed and number == 0:
            arrived[2], *pieces = gate([arrived[2], *here[3][1:], *here[1][1:]], [near])
            here[3][1:], here[1][1:] = pieces[: tensors - 1], pieces[tensors - 1 :]
            here[2] = across(2)
        elif relayed and number == 1:
            both = gate([*far, *here[2][1:]], [])
            far, here[2][1:] = both[: len(far)], both[len(far) :]
        elif relayed and number == 2:
            last = [pair for pair, _ in came[3]]
        count = len(chunk)
        added = add_split(near, [swap(block, "expert", 1) for block in far], count, last)
        if len(chunk) > 1:
            pairs = [swap(block, "tensor", j + 1) for j, block in enumerate(added[count:])]
            for i, k in enumerate(chunk):
                sums[k] = added[i]
                came[k] = [(pair, i) for pair in pairs]
            continue
        for i, k in enumerate(chunk):
            sums[k] = added[i]
            sent = [added[j * count + i] for j in range(1, tensors)]
            if relayed and k == 0:
                held[k] = sent
            else:
                came[k] = [swap(piece, "tensor", j + 1) for j, piece in enumerate(sent)]
    if relayed:
        held[0] = gate(held[0], came[2])
        came[0] = [swap(piece, "tensor", j + 1) for j, piece in enumerate(held[0])]

    def back(k, more=(), after=()):
        distance = 1 if relayed and k == 3 else k
        return swap(add_up([sums[k], *came[k], *more], BF16, after), "expert", 2 * distance)

    relay = [back(3)] if relayed else []
    terms = [sums[0], *came[0]]
    for k in order[1:]:
        if not relayed or k != 3:
            terms.append(back(k, relay if k == 2 else (), relay if k == 1 else ()))
    return add_up(terms, BF16)


def solution(mesh):
    return jax.shard_map(
        functools.partial(per_device, (mesh.shape["expert"], mesh.shape["tensor"])),
        mesh=mesh,
        in_specs=(
            P(("group", "expert"), "tensor"),
            P("tensor", None),
            P(),
            P("expert", None, None, "tensor"),
            P("expert", "tensor", None),
            P(("group", "expert", "tensor"), None),
            P(("group", "expert", "tensor"), None),
        ),
        out_specs=P(("group", "expert", "tensor"), None),
        check_vma=False,
    )
```

```python
import functools

import jax
import jax.numpy as jnp
from jax import lax
from jax.experimental import pallas as pl
from jax.experimental.pallas import tpu as pltpu
from jax.sharding import PartitionSpec as P

F32 = jnp.float32
BF16 = jnp.bfloat16
NT = (((1,), (1,)), ((), ()))
TN = (((0,), (0,)), ((), ()))

AHEAD = 2
CHEAP = pl.CostEstimate(flops=0, bytes_accessed=0, transcendentals=0)


def project_kernel(tile, tensor_ref, heads_hbm, w_hbm, *refs):
    *part_refs, heads_ref, w_ref, out_ref, heads_sem, sems = refs
    width, depth = w_ref.shape
    first = pltpu.make_async_copy(heads_hbm, heads_ref, heads_sem)
    first.start()
    tiles = [(start, min(tile, width - start)) for start in range(0, width, tile)]
    copies = []
    for i, (start, size) in enumerate(tiles):
        rows = pl.ds(start, size)
        copies.append(pltpu.make_async_copy(w_hbm.at[rows], w_ref.at[rows], sems.at[i]))
    for copy in copies[:AHEAD]:
        copy.start()
    first.wait()
    heads = heads_ref[...]
    for i, (start, size) in enumerate(tiles):
        copies[i].wait()
        if i + AHEAD < len(tiles):
            copies[i + AHEAD].start()
        out = lax.dot_general(heads, w_ref[start : start + size], NT, preferred_element_type=F32)
        out_ref[:, start : start + size] = out.astype(BF16)
    tokens = part_refs[0].shape[0]
    for j, part_ref in enumerate(part_refs):
        start = pl.multiple_of((tensor_ref[0] ^ j) * tokens, tokens)
        part_ref[...] = out_ref[pl.ds(start, tokens)]


def project(tensor, heads_out, out_proj_t, tensors):
    rows, depth = heads_out.shape
    width = out_proj_t.shape[0]
    tile = 512
    hbm = pl.BlockSpec(memory_space=pltpu.HBM)
    part = jax.ShapeDtypeStruct((rows // tensors, width), BF16)
    return pl.pallas_call(
        functools.partial(project_kernel, tile),
        in_specs=[pl.BlockSpec(memory_space=pltpu.SMEM), hbm, hbm],
        out_specs=[pl.BlockSpec(memory_space=pltpu.VMEM)] * tensors,
        out_shape=[part] * tensors,
        scratch_shapes=[
            pltpu.VMEM((rows, depth), BF16),
            pltpu.VMEM((width, depth), BF16),
            pltpu.VMEM((rows, width), BF16),
            pltpu.SemaphoreType.DMA,
            pltpu.SemaphoreType.DMA((pl.cdiv(width, tile),)),
        ],
        compiler_params=pltpu.CompilerParams(vmem_limit_bytes=24 * 2**20),
        cost_estimate=CHEAP,
        name="project",
    )(
        tensor,
        pltpu.with_memory_space_constraint(heads_out, pltpu.HBM),
        pltpu.with_memory_space_constraint(out_proj_t, pltpu.HBM),
    )


def norm_kernel(experts, *refs):
    *parts, gain_ref, routes_ref, weights_ref, _, out_ref = refs
    hidden = parts[0][...].astype(F32)
    for part in parts[1:]:
        hidden = hidden + part[...].astype(F32)
    rows, width = hidden.shape
    scale = lax.rsqrt(jnp.mean(hidden * hidden, axis=1, keepdims=True) + 1e-05)
    out_ref[:, :width] = (hidden * scale * gain_ref[...]).astype(BF16)
    extra = out_ref.shape[1] - width
    column = lax.broadcasted_iota(jnp.int32, (rows, extra), 1)
    expert, term = lax.rem(column, experts), lax.div(column, experts)
    weight = jnp.zeros((rows, extra), F32)
    for k in range(routes_ref.shape[1]):
        weight = weight + jnp.where(routes_ref[:, k : k + 1] == expert, weights_ref[:, k : k + 1], 0.0)
    high = weight.astype(BF16).astype(F32)
    middle = (weight - high).astype(BF16).astype(F32)
    low = weight - high - middle
    out_ref[:, width:] = jnp.where(
        term == 0, high, jnp.where(term == 1, middle, jnp.where(term == 2, low, 0.0))
    ).astype(BF16)


def expert_kernel(experts, pieces, outputs, expert_ref, *refs):
    tokens = refs[:pieces]
    w_in_ref, w_out_ref = refs[pieces : pieces + 2]
    near_ref, *far_refs, act_ref = refs[outputs:]
    hidden, width = w_out_ref.shape
    block = jnp.concatenate([piece[...].reshape(-1, piece.shape[-1]) for piece in tokens], axis=0)
    x, extra = block[:, :width], block[:, width:].astype(F32)
    column = lax.broadcasted_iota(jnp.int32, extra.shape, 1)
    mine = (lax.rem(column, experts) == expert_ref[0]) & (column < 3 * experts)
    weight = jnp.sum(jnp.where(mine, extra, 0.0), axis=1, keepdims=True)
    step = 480 if hidden % 480 == 0 else hidden
    for start in range(0, hidden, step):
        gate = lax.dot_general(w_in_ref[0, start : start + step], x, NT, preferred_element_type=F32)
        up = lax.dot_general(w_in_ref[1, start : start + step], x, NT, preferred_element_type=F32)
        act = gate * jax.nn.sigmoid(1.702 * gate) * (up + 1.0)
        act_ref[start : start + step, :] = act.astype(BF16)
    out = lax.dot_general(act_ref[...], w_out_ref[...], TN, preferred_element_type=F32) * weight
    half = out.shape[0] // 2
    near_ref[...] = out[:half].astype(BF16).reshape(near_ref.shape)
    far = out[half:].astype(BF16)
    size = half // len(far_refs)
    for i, far_ref in enumerate(far_refs):
        far_ref[...] = far[i * size : (i + 1) * size].reshape(far_ref.shape)


def expert_chunk(expert, tokens, w_in, w_out, experts, after, split):
    rows = sum(piece.size // piece.shape[-1] for piece in tokens)
    hidden, width = w_out.shape
    vmem = pl.BlockSpec(memory_space=pltpu.VMEM)
    unit = tokens[0].shape[0]
    blocks = rows // 2 // unit
    near = jax.ShapeDtypeStruct((blocks, unit, width), BF16)
    far = [jax.ShapeDtypeStruct((unit, width), BF16)] * blocks if split else [near]
    inputs = len(tokens) + 2 + len(after)
    return pl.pallas_call(
        functools.partial(expert_kernel, experts, len(tokens), inputs),
        in_specs=[pl.BlockSpec(memory_space=pltpu.SMEM)]
        + [vmem] * (len(tokens) + 2)
        + [pl.BlockSpec(memory_space=pl.ANY)] * len(after),
        out_specs=[vmem] * (1 + len(far)),
        out_shape=[near, *far],
        scratch_shapes=[pltpu.VMEM((hidden, rows), BF16)],
        compiler_params=pltpu.CompilerParams(vmem_limit_bytes=24 * 2**20),
        cost_estimate=pl.CostEstimate(
            flops=6 * rows * hidden * width, bytes_accessed=rows * width, transcendentals=rows * hidden
        ),
        name="expert",
    )(
        expert,
        *tokens,
        pltpu.with_memory_space_constraint(w_in, pltpu.VMEM),
        pltpu.with_memory_space_constraint(w_out, pltpu.VMEM),
        *after,
    )


def load_kernel(source_ref, *refs):
    target_ref, token_ref, sem = refs[-3:]
    copy = pltpu.make_async_copy(source_ref, target_ref, sem)
    copy.start()
    token_ref[...] = jnp.zeros_like(token_ref)
    copy.wait()


def load(weights, after):
    return pl.pallas_call(
        load_kernel,
        in_specs=[pl.BlockSpec(memory_space=pltpu.HBM)] + [pl.BlockSpec(memory_space=pl.ANY)] * len(after),
        out_specs=[pl.BlockSpec(memory_space=pltpu.VMEM)] * 2,
        out_shape=[pltpu.VMEM(weights.shape, weights.dtype), jax.ShapeDtypeStruct((8, 128), F32)],
        scratch_shapes=[pltpu.SemaphoreType.DMA],
        compiler_params=pltpu.CompilerParams(vmem_limit_bytes=2**20),
        cost_estimate=pl.CostEstimate(flops=0, bytes_accessed=2 * weights.size, transcendentals=0),
        name="load",
    )(pltpu.with_memory_space_constraint(weights, pltpu.HBM), *after)


def add_kernel(fars, outputs, near_ref, *refs):
    far_refs = refs[:fars]

    def block(i):
        far = far_refs[0][i] if fars == 1 else far_refs[i][...]
        return near_ref[i].astype(F32) + far.astype(F32)

    done = 0
    for out_ref in refs[-outputs:]:
        if len(out_ref.shape) == 2:
            out_ref[...] = block(done).astype(out_ref.dtype)
            done += 1
        else:
            for i in range(out_ref.shape[0]):
                out_ref[i] = block(done).astype(out_ref.dtype)
                done += 1


def add_split(near, fars, kept, after):
    blocks, *shape = near.shape
    vmem = pl.BlockSpec(memory_space=pltpu.VMEM)
    sent = shape if kept == 1 else (kept, *shape)
    shapes = [jax.ShapeDtypeStruct(shape, F32)] * kept + [jax.ShapeDtypeStruct(sent, BF16)] * (blocks // kept - 1)
    return pl.pallas_call(
        functools.partial(add_kernel, len(fars), len(shapes)),
        in_specs=[vmem] * (1 + len(fars)) + [pl.BlockSpec(memory_space=pl.ANY)] * len(after),
        out_specs=[vmem] * len(shapes),
        out_shape=shapes,
        compiler_params=pltpu.CompilerParams(vmem_limit_bytes=16 * 2**20),
        cost_estimate=CHEAP,
        name="add_split",
    )(near, *fars, *after)


def gate_kernel(count, *refs):
    for source_ref, out_ref in zip(refs[:count], refs[len(refs) - count :]):
        out_ref[...] = source_ref[...]


def gate(values, after):
    vmem = pl.BlockSpec(memory_space=pltpu.VMEM)
    return pl.pallas_call(
        functools.partial(gate_kernel, len(values)),
        in_specs=[vmem] * len(values) + [pl.BlockSpec(memory_space=pl.ANY)] * len(after),
        out_specs=[vmem] * len(values),
        out_shape=[jax.ShapeDtypeStruct(value.shape, value.dtype) for value in values],
        compiler_params=pltpu.CompilerParams(vmem_limit_bytes=4 * 2**20),
        cost_estimate=CHEAP,
        name="gate",
    )(*values, *after)


def stack_kernel(first_ref, second_ref, other_ref, *refs):
    pair_ref, copy_ref = refs[-2:]
    pair_ref[0], pair_ref[1] = first_ref[...], second_ref[...]
    copy_ref[...] = other_ref[...]


def stack(first, second, other, after):
    vmem = pl.BlockSpec(memory_space=pltpu.VMEM)
    return pl.pallas_call(
        stack_kernel,
        in_specs=[vmem] * 3 + [pl.BlockSpec(memory_space=pl.ANY)] * len(after),
        out_specs=[vmem] * 2,
        out_shape=[
            jax.ShapeDtypeStruct((2, *first.shape), first.dtype),
            jax.ShapeDtypeStruct(other.shape, other.dtype),
        ],
        compiler_params=pltpu.CompilerParams(vmem_limit_bytes=4 * 2**20),
        cost_estimate=CHEAP,
        name="stack",
    )(first, second, other, *after)


def sum_kernel(places, *refs):
    total = None
    for place, ref in zip(places, refs):
        term = (ref[...] if place is None else ref[place]).astype(F32)
        total = term if total is None else total + term
    refs[-1][...] = total.astype(refs[-1].dtype)


def add_up(terms, dtype, after=()):
    vmem = pl.BlockSpec(memory_space=pltpu.VMEM)
    places = [term[1] if isinstance(term, tuple) else None for term in terms]
    arrays = [term[0] if isinstance(term, tuple) else term for term in terms]
    return pl.pallas_call(
        functools.partial(sum_kernel, places),
        in_specs=[vmem] * len(terms) + [pl.BlockSpec(memory_space=pl.ANY)] * len(after),
        out_specs=vmem,
        out_shape=jax.ShapeDtypeStruct(arrays[0].shape, dtype),
        compiler_params=pltpu.CompilerParams(vmem_limit_bytes=16 * 2**20),
        cost_estimate=CHEAP,
        name="add_up",
    )(*arrays, *after)


def per_device(sizes, heads_out, out_proj, norm_gain, gate_up, down_proj, routes, gate_weights):
    experts, tensors = sizes
    tokens = routes.shape[0]
    width = out_proj.shape[1]
    padded = -(-(width + 3 * experts) // 128) * 128
    expert = lax.axis_index("expert")
    tensor = lax.axis_index("tensor")

    def swap(values, axis, distance):
        pairs = [(i, i ^ distance) for i in range(lax.axis_size(axis))]
        return lax.ppermute(values, axis, pairs)

    mine, *sent = project(tensor.reshape(1), heads_out, out_proj.T, tensors)
    gain = norm_gain.reshape(1, width)
    me = expert.reshape(1)
    w_in, w_in_there = load(gate_up[0].transpose(1, 2, 0), [*sent, gain, routes, gate_weights, me])
    parts = [mine] + [swap(sent[j - 1], "tensor", j) for j in range(1, tensors)]
    own = pl.pallas_call(
        functools.partial(norm_kernel, experts),
        in_specs=[pl.BlockSpec(memory_space=pltpu.VMEM)] * (tensors + 3) + [pl.BlockSpec(memory_space=pl.ANY)],
        out_shape=jax.ShapeDtypeStruct((tokens, padded), BF16),
        compiler_params=pltpu.CompilerParams(vmem_limit_bytes=8 * 2**20),
        name="norm",
    )(*parts, gain, routes, gate_weights, w_in_there)
    w_out, w_out_there = load(down_proj[0], [own])

    chips = experts // 2
    relayed = chips > 3
    order = [0, 1, 3, 2, *range(4, chips)][:chips] if relayed else list(range(chips))
    arrived = {0: own}
    for k in order[1:]:
        if relayed and k == 2:
            arrived[k] = swap(arrived[3], "expert", 2)
        else:
            arrived[k] = swap(own, "expert", 2 * k)
        if k == 1:
            (arrived[k],) = gate([arrived[k]], [w_out_there])
    chunks = [[0], [1, 3], *([k] for k in order[3:])] if relayed else [[k] for k in order]

    def across(k):
        return [arrived[k]] + [swap(arrived[k], "tensor", j) for j in range(1, tensors)]

    here = {k: across(k) for k in order if not relayed or k != 2}
    sums, came, held = {}, {}, {}
    for number, chunk in enumerate(chunks):
        ordered = [here[k][j] for j in range(tensors) for k in chunk]
        ordered += [swap(here[k][0], "expert", 1) for k in chunk]
        if len(chunk) > 1:
            ordered += [swap(pair, "expert", 1) for pair in stacked]
        else:
            ordered += [swap(piece, "expert", 1) for piece in here[chunk[0]][1:]]
        after = [arrived[3]] if relayed and number == 0 else []
        near, *far = expert_chunk(me, ordered, w_in, w_out, experts, after, relayed and number == 2)
        last = []
        if relayed and number == 0:
            stacked = []
            for j in range(1, tensors):
                pair, arrived[2] = stack(here[1][j], here[3][j], arrived[2], [near])
                stacked.append(pair)
            here[2] = across(2)
        elif relayed and number == 1:
            both = gate([*far, *here[2][1:]], [])
            far, here[2][1:] = both[: len(far)], both[len(far) :]
        elif relayed and number == 2:
            last = [pair for pair, _ in came[3]]
        count = len(chunk)
        added = add_split(near, [swap(block, "expert", 1) for block in far], count, last)
        if len(chunk) > 1:
            pairs = [swap(block, "tensor", j + 1) for j, block in enumerate(added[count:])]
            for i, k in enumerate(chunk):
                sums[k] = added[i]
                came[k] = [(pair, i) for pair in pairs]
            continue
        for i, k in enumerate(chunk):
            sums[k] = added[i]
            sent = [added[j * count + i] for j in range(1, tensors)]
            if relayed and k == 0:
                held[k] = sent
            else:
                came[k] = [swap(piece, "tensor", j + 1) for j, piece in enumerate(sent)]
    if relayed:
        held[0] = gate(held[0], came[2])
        came[0] = [swap(piece, "tensor", j + 1) for j, piece in enumerate(held[0])]

    def back(k, more=(), after=()):
        distance = 1 if relayed and k == 3 else k
        return swap(add_up([sums[k], *came[k], *more], BF16, after), "expert", 2 * distance)

    relay = [back(3)] if relayed else []
    terms = [sums[0], *came[0]]
    for k in order[1:]:
        if not relayed or k != 3:
            terms.append(back(k, relay if k == 2 else (), relay if k == 1 else ()))
    return add_up(terms, BF16)


def solution(mesh):
    return jax.shard_map(
        functools.partial(per_device, (mesh.shape["expert"], mesh.shape["tensor"])),
        mesh=mesh,
        in_specs=(
            P(("group", "expert"), "tensor"),
            P("tensor", None),
            P(),
            P("expert", None, None, "tensor"),
            P("expert", "tensor", None),
            P(("group", "expert", "tensor"), None),
            P(("group", "expert", "tensor"), None),
        ),
        out_specs=P(("group", "expert", "tensor"), None),
        check_vma=False,
    )
```

```python
import functools

import jax
import jax.numpy as jnp
from jax import lax
from jax.experimental import pallas as pl
from jax.experimental.pallas import tpu as pltpu
from jax.sharding import PartitionSpec as P

F32 = jnp.float32
BF16 = jnp.bfloat16
NT = (((1,), (1,)), ((), ()))
TN = (((0,), (0,)), ((), ()))

AHEAD = 2
CHEAP = pl.CostEstimate(flops=0, bytes_accessed=0, transcendentals=0)


def project_kernel(tile, tensor_ref, heads_hbm, w_hbm, *refs):
    *part_refs, heads_ref, w_ref, out_ref, heads_sem, sems = refs
    width, depth = w_ref.shape
    first = pltpu.make_async_copy(heads_hbm, heads_ref, heads_sem)
    first.start()
    tiles = [(start, min(tile, width - start)) for start in range(0, width, tile)]
    copies = []
    for i, (start, size) in enumerate(tiles):
        rows = pl.ds(start, size)
        copies.append(pltpu.make_async_copy(w_hbm.at[rows], w_ref.at[rows], sems.at[i]))
    for copy in copies[:AHEAD]:
        copy.start()
    first.wait()
    heads = heads_ref[...]
    for i, (start, size) in enumerate(tiles):
        copies[i].wait()
        if i + AHEAD < len(tiles):
            copies[i + AHEAD].start()
        half = depth // 2
        out = lax.dot_general(heads[:, :half], w_ref[start : start + size, :half], NT, preferred_element_type=F32)
        out = out + lax.dot_general(heads[:, half:], w_ref[start : start + size, half:], NT, preferred_element_type=F32)
        out_ref[:, start : start + size] = out.astype(BF16)
    tokens = part_refs[0].shape[0]
    for j, part_ref in enumerate(part_refs):
        start = pl.multiple_of((tensor_ref[0] ^ j) * tokens, tokens)
        part_ref[...] = out_ref[pl.ds(start, tokens)]


def project(tensor, heads_out, out_proj_t, tensors):
    rows, depth = heads_out.shape
    width = out_proj_t.shape[0]
    tile = 512
    hbm = pl.BlockSpec(memory_space=pltpu.HBM)
    part = jax.ShapeDtypeStruct((rows // tensors, width), BF16)
    return pl.pallas_call(
        functools.partial(project_kernel, tile),
        in_specs=[pl.BlockSpec(memory_space=pltpu.SMEM), hbm, hbm],
        out_specs=[pl.BlockSpec(memory_space=pltpu.VMEM)] * tensors,
        out_shape=[part] * tensors,
        scratch_shapes=[
            pltpu.VMEM((rows, depth), BF16),
            pltpu.VMEM((width, depth), BF16),
            pltpu.VMEM((rows, width), BF16),
            pltpu.SemaphoreType.DMA,
            pltpu.SemaphoreType.DMA((pl.cdiv(width, tile),)),
        ],
        compiler_params=pltpu.CompilerParams(vmem_limit_bytes=24 * 2**20),
        cost_estimate=CHEAP,
        name="project",
    )(
        tensor,
        pltpu.with_memory_space_constraint(heads_out, pltpu.HBM),
        pltpu.with_memory_space_constraint(out_proj_t, pltpu.HBM),
    )


def norm_kernel(experts, *refs):
    *parts, gain_ref, routes_ref, weights_ref, _, out_ref = refs
    hidden = parts[0][...].astype(F32)
    for part in parts[1:]:
        hidden = hidden + part[...].astype(F32)
    rows, width = hidden.shape
    scale = lax.rsqrt(jnp.mean(hidden * hidden, axis=1, keepdims=True) + 1e-05)
    out_ref[:, :width] = (hidden * scale * gain_ref[...]).astype(BF16)
    extra = out_ref.shape[1] - width
    column = lax.broadcasted_iota(jnp.int32, (rows, extra), 1)
    expert, term = lax.rem(column, experts), lax.div(column, experts)
    weight = jnp.zeros((rows, extra), F32)
    for k in range(routes_ref.shape[1]):
        weight = weight + jnp.where(routes_ref[:, k : k + 1] == expert, weights_ref[:, k : k + 1], 0.0)
    high = weight.astype(BF16).astype(F32)
    middle = (weight - high).astype(BF16).astype(F32)
    low = weight - high - middle
    out_ref[:, width:] = jnp.where(
        term == 0, high, jnp.where(term == 1, middle, jnp.where(term == 2, low, 0.0))
    ).astype(BF16)


def expert_kernel(experts, pieces, outputs, expert_ref, *refs):
    tokens = refs[:pieces]
    w_in_ref, w_out_ref = refs[pieces : pieces + 2]
    near_ref, *far_refs, act_ref = refs[outputs:]
    hidden, width = w_out_ref.shape
    block = jnp.concatenate([piece[...] for piece in tokens], axis=0)
    x, extra = block[:, :width], block[:, width:].astype(F32)
    column = lax.broadcasted_iota(jnp.int32, extra.shape, 1)
    mine = (lax.rem(column, experts) == expert_ref[0]) & (column < 3 * experts)
    weight = jnp.sum(jnp.where(mine, extra, 0.0), axis=1, keepdims=True)
    step = 480 if hidden % 480 == 0 else hidden
    for start in range(0, hidden, step):
        gate = lax.dot_general(w_in_ref[0, start : start + step], x, NT, preferred_element_type=F32)
        up = lax.dot_general(w_in_ref[1, start : start + step], x, NT, preferred_element_type=F32)
        act = gate * jax.nn.sigmoid(1.702 * gate) * (up + 1.0)
        act_ref[start : start + step, :] = act.astype(BF16)
    out = lax.dot_general(act_ref[...], w_out_ref[...], TN, preferred_element_type=F32) * weight
    half = out.shape[0] // 2
    near_ref[...] = out[:half].astype(BF16).reshape(near_ref.shape)
    far = out[half:].astype(BF16)
    size = half // len(far_refs)
    for i, far_ref in enumerate(far_refs):
        far_ref[...] = far[i * size : (i + 1) * size].reshape(far_ref.shape)


def expert_chunk(expert, tokens, w_in, w_out, experts, after, split):
    rows = sum(piece.shape[0] for piece in tokens)
    hidden, width = w_out.shape
    vmem = pl.BlockSpec(memory_space=pltpu.VMEM)
    unit = tokens[0].shape[0]
    blocks = rows // 2 // unit
    near = jax.ShapeDtypeStruct((blocks, unit, width), BF16)
    far = [jax.ShapeDtypeStruct((unit, width), BF16)] * blocks if split else [near]
    inputs = len(tokens) + 2 + len(after)
    return pl.pallas_call(
        functools.partial(expert_kernel, experts, len(tokens), inputs),
        in_specs=[pl.BlockSpec(memory_space=pltpu.SMEM)]
        + [vmem] * (len(tokens) + 2)
        + [pl.BlockSpec(memory_space=pl.ANY)] * len(after),
        out_specs=[vmem] * (1 + len(far)),
        out_shape=[near, *far],
        scratch_shapes=[pltpu.VMEM((hidden, rows), BF16)],
        compiler_params=pltpu.CompilerParams(vmem_limit_bytes=24 * 2**20),
        cost_estimate=pl.CostEstimate(
            flops=6 * rows * hidden * width, bytes_accessed=rows * width, transcendentals=rows * hidden
        ),
        name="expert",
    )(
        expert,
        *tokens,
        pltpu.with_memory_space_constraint(w_in, pltpu.VMEM),
        pltpu.with_memory_space_constraint(w_out, pltpu.VMEM),
        *after,
    )


def load_kernel(source_ref, *refs):
    target_ref, token_ref, sem = refs[-3:]
    copy = pltpu.make_async_copy(source_ref, target_ref, sem)
    copy.start()
    token_ref[...] = jnp.zeros_like(token_ref)
    copy.wait()


def load(weights, after):
    return pl.pallas_call(
        load_kernel,
        in_specs=[pl.BlockSpec(memory_space=pltpu.HBM)] + [pl.BlockSpec(memory_space=pl.ANY)] * len(after),
        out_specs=[pl.BlockSpec(memory_space=pltpu.VMEM)] * 2,
        out_shape=[pltpu.VMEM(weights.shape, weights.dtype), jax.ShapeDtypeStruct((8, 128), F32)],
        scratch_shapes=[pltpu.SemaphoreType.DMA],
        compiler_params=pltpu.CompilerParams(vmem_limit_bytes=2**20),
        cost_estimate=pl.CostEstimate(flops=0, bytes_accessed=2 * weights.size, transcendentals=0),
        name="load",
    )(pltpu.with_memory_space_constraint(weights, pltpu.HBM), *after)


def add_kernel(fars, outputs, near_ref, *refs):
    far_refs = refs[:fars]

    def block(i):
        far = far_refs[0][i] if fars == 1 else far_refs[i][...]
        return near_ref[i].astype(F32) + far.astype(F32)

    done = 0
    for out_ref in refs[-outputs:]:
        if len(out_ref.shape) == 2:
            out_ref[...] = block(done).astype(out_ref.dtype)
            done += 1
        else:
            for i in range(out_ref.shape[0]):
                out_ref[i] = block(done).astype(out_ref.dtype)
                done += 1


def add_split(near, fars, kept, after):
    blocks, *shape = near.shape
    vmem = pl.BlockSpec(memory_space=pltpu.VMEM)
    sent = shape if kept == 1 else (kept, *shape)
    shapes = [jax.ShapeDtypeStruct(shape, F32)] * kept + [jax.ShapeDtypeStruct(sent, BF16)] * (blocks // kept - 1)
    return pl.pallas_call(
        functools.partial(add_kernel, len(fars), len(shapes)),
        in_specs=[vmem] * (1 + len(fars)) + [pl.BlockSpec(memory_space=pl.ANY)] * len(after),
        out_specs=[vmem] * len(shapes),
        out_shape=shapes,
        compiler_params=pltpu.CompilerParams(vmem_limit_bytes=16 * 2**20),
        cost_estimate=CHEAP,
        name="add_split",
    )(near, *fars, *after)


def gate_kernel(count, *refs):
    for source_ref, out_ref in zip(refs[:count], refs[len(refs) - count :]):
        out_ref[...] = source_ref[...]


def gate(values, after):
    vmem = pl.BlockSpec(memory_space=pltpu.VMEM)
    return pl.pallas_call(
        functools.partial(gate_kernel, len(values)),
        in_specs=[vmem] * len(values) + [pl.BlockSpec(memory_space=pl.ANY)] * len(after),
        out_specs=[vmem] * len(values),
        out_shape=[jax.ShapeDtypeStruct(value.shape, value.dtype) for value in values],
        compiler_params=pltpu.CompilerParams(vmem_limit_bytes=4 * 2**20),
        cost_estimate=CHEAP,
        name="gate",
    )(*values, *after)


def sum_kernel(places, *refs):
    total = None
    for place, ref in zip(places, refs):
        term = (ref[...] if place is None else ref[place]).astype(F32)
        total = term if total is None else total + term
    refs[-1][...] = total.astype(refs[-1].dtype)


def add_up(terms, dtype, after=()):
    vmem = pl.BlockSpec(memory_space=pltpu.VMEM)
    places = [term[1] if isinstance(term, tuple) else None for term in terms]
    arrays = [term[0] if isinstance(term, tuple) else term for term in terms]
    return pl.pallas_call(
        functools.partial(sum_kernel, places),
        in_specs=[vmem] * len(terms) + [pl.BlockSpec(memory_space=pl.ANY)] * len(after),
        out_specs=vmem,
        out_shape=jax.ShapeDtypeStruct(arrays[0].shape, dtype),
        compiler_params=pltpu.CompilerParams(vmem_limit_bytes=16 * 2**20),
        cost_estimate=CHEAP,
        name="add_up",
    )(*arrays, *after)


def per_device(sizes, heads_out, out_proj, norm_gain, gate_up, down_proj, routes, gate_weights):
    experts, tensors = sizes
    tokens = routes.shape[0]
    width = out_proj.shape[1]
    padded = -(-(width + 3 * experts) // 128) * 128
    expert = lax.axis_index("expert")
    tensor = lax.axis_index("tensor")

    def swap(values, axis, distance):
        pairs = [(i, i ^ distance) for i in range(lax.axis_size(axis))]
        return lax.ppermute(values, axis, pairs)

    mine, *sent = project(tensor.reshape(1), heads_out, out_proj.T, tensors)
    gain = norm_gain.reshape(1, width)
    me = expert.reshape(1)
    w_in, w_in_there = load(gate_up[0].transpose(1, 2, 0), [*sent, gain, routes, gate_weights, me])
    parts = [mine] + [swap(sent[j - 1], "tensor", j) for j in range(1, tensors)]
    own = pl.pallas_call(
        functools.partial(norm_kernel, experts),
        in_specs=[pl.BlockSpec(memory_space=pltpu.VMEM)] * (tensors + 3) + [pl.BlockSpec(memory_space=pl.ANY)],
        out_shape=jax.ShapeDtypeStruct((tokens, padded), BF16),
        compiler_params=pltpu.CompilerParams(vmem_limit_bytes=8 * 2**20),
        name="norm",
    )(*parts, gain, routes, gate_weights, w_in_there)
    w_out, w_out_there = load(down_proj[0], [own])

    chips = experts // 2
    relayed = chips > 3
    order = [0, 1, 3, 2, *range(4, chips)][:chips] if relayed else list(range(chips))
    arrived = {0: own}
    for k in order[1:]:
        if relayed and k == 2:
            arrived[k] = swap(arrived[3], "expert", 2)
        else:
            arrived[k] = swap(own, "expert", 2 * k)
        if k == 1:
            (arrived[k],) = gate([arrived[k]], [w_out_there])
    chunks = [[0], [1, 3], *([k] for k in order[3:])] if relayed else [[k] for k in order]

    def across(k):
        return [arrived[k]] + [swap(arrived[k], "tensor", j) for j in range(1, tensors)]

    here = {k: across(k) for k in order if not relayed or k != 2}
    sums, came, held = {}, {}, {}
    for number, chunk in enumerate(chunks):
        there = {k: [swap(piece, "expert", 1) for piece in here[k]] for k in chunk}
        ordered = [side[k][j] for side in (here, there) for j in range(tensors) for k in chunk]
        after = [arrived[3]] if relayed and number == 0 else []
        near, *far = expert_chunk(me, ordered, w_in, w_out, experts, after, relayed and number == 2)
        last = []
        if relayed and number == 0:
            arrived[2], *pieces = gate([arrived[2], *here[3][1:], *here[1][1:]], [near])
            here[3][1:], here[1][1:] = pieces[: tensors - 1], pieces[tensors - 1 :]
            here[2] = across(2)
        elif relayed and number == 1:
            both = gate([*far, *here[2][1:]], [])
            far, here[2][1:] = both[: len(far)], both[len(far) :]
        elif relayed and number == 2:
            last = [pair for pair, _ in came[3]]
        count = len(chunk)
        added = add_split(near, [swap(block, "expert", 1) for block in far], count, last)
        if len(chunk) > 1:
            pairs = [swap(block, "tensor", j + 1) for j, block in enumerate(added[count:])]
            for i, k in enumerate(chunk):
                sums[k] = added[i]
                came[k] = [(pair, i) for pair in pairs]
            continue
        for i, k in enumerate(chunk):
            sums[k] = added[i]
            sent = [added[j * count + i] for j in range(1, tensors)]
            if relayed and k == 0:
                held[k] = sent
            else:
                came[k] = [swap(piece, "tensor", j + 1) for j, piece in enumerate(sent)]
    if relayed:
        held[0] = gate(held[0], came[2])
        came[0] = [swap(piece, "tensor", j + 1) for j, piece in enumerate(held[0])]

    def back(k, more=(), after=()):
        distance = 1 if relayed and k == 3 else k
        return swap(add_up([sums[k], *came[k], *more], BF16, after), "expert", 2 * distance)

    relay = [back(3)] if relayed else []
    terms = [sums[0], *came[0]]
    for k in order[1:]:
        if not relayed or k != 3:
            terms.append(back(k, relay if k == 2 else (), relay if k == 1 else ()))
    return add_up(terms, BF16)


def solution(mesh):
    return jax.shard_map(
        functools.partial(per_device, (mesh.shape["expert"], mesh.shape["tensor"])),
        mesh=mesh,
        in_specs=(
            P(("group", "expert"), "tensor"),
            P("tensor", None),
            P(),
            P("expert", None, None, "tensor"),
            P("expert", "tensor", None),
            P(("group", "expert", "tensor"), None),
            P(("group", "expert", "tensor"), None),
        ),
        out_specs=P(("group", "expert", "tensor"), None),
        check_vma=False,
    )
```
